1024 devices in a mesh: row: 128 (over y_hi, x, z), rep: 8 (over y_lo, core).
Axes of the slice: x: 4, y: 8 (y_hi: 2, y_lo: 4; y = y_hi * 4 + y_lo), z: 16, core: 2. Of those that a mesh axis runs over, the one named last changes fastest.
Arguments:
- features: bfloat16 [131072, 256], P(('row', 'rep')), may hold values from -6 to 6
- weight: bfloat16 [256, 256], replicated, may hold values from -0.375 to 0.375
- bias: float32 [256], replicated, may hold values from -3 to 3
- dense_adj: bfloat16 [128, 8, 5, 1024, 128], P('row', 'rep'), may hold values from -0.078125 to 0.078125
- dense_mask: int32 [128, 8, 5, 8, 1], P('row', 'rep'), may hold values 0 or 1
- sparse_adj: bfloat16 [128, 8, 1024, 768], P('row', 'rep'), may hold values from -0.078125 to 0.078125
- sparse_cols: int32 [128, 8, 6], P('row', 'rep'), may hold values from 0 to 7
- sparse_count: int32 [128, 8], P('row', 'rep'), may hold values from 1 to 6, as said below
- cotangent: bfloat16 [131072, 256], P(('row', 'rep')), may hold values from -0.015625 to 0.015625
Outputs:
- activated: bfloat16 [131072, 256], P(('row', 'rep'))
- weight_grad: float32 [256, 256], replicated
- bias_grad: float32 [256], replicated
The draws below stay inside these ranges and needn't reach their ends.
Inputs may be any that keep to these rules, and one draw needn't show every extreme that they name: `sparse_count`: some device has all 6 slots live.
All inputs are finite; a program needn't handle non-finite values. No bound on the sum of `dense_mask` on one device may be relied on, other than what follows from the above.
Results may differ from the reference program's by a relative error of at most 0.017.
Values may be sent and summed in bfloat16 or wider, within the bound.
No kernel may reach another device: no remote copies, remote signals or barrier semaphores. Data moves between devices by JAX's collectives and lax.ppermute only.
A program may use at most 32 MiB of HBM per device.

```python
import jax
import jax.numpy as jnp
from jax import lax

F = 256
BLK = 128
H = 2
SPMAX = 6
RS = 128
BAND = 5
PANEL = 1024
NODES = 131072
N_ROW = 128
N_REP = 8


def draw_sparse_count(key, part):
    key = jax.random.fold_in(key, 7)
    counts = jax.random.randint(key, (N_ROW, N_REP), 1, SPMAX + 1)
    return counts.at[0, 0].set(SPMAX).astype(jnp.int32)


def with_ends(result, own_key, smallest, largest):
    place = [jax.random.randint(jax.random.fold_in(own_key, axis), (), 0, length) for axis, length in enumerate(result.shape)]
    widest = result.shape.index(max(result.shape))
    neighbour = place[:widest] + [(place[widest] + 1) % result.shape[widest]] + place[widest + 1:]
    return result.at[tuple(place)].set(smallest).at[tuple(neighbour)].set(largest)


def level_of(own_key, shape, shards, smallest, high):
    gain, own = 1.0, jax.random.fold_in(own_key, 6)
    for position, parts in shards:
        heights = jnp.exp(jax.random.uniform(jax.random.fold_in(own, position), (parts,), jnp.float32, smallest / len(shards), high / len(shards)))
        gain = gain * jnp.repeat(heights, shape[position] // parts).reshape([-1 if axis == position else 1 for axis in range(len(shape))])
    return gain


def centred(own_key, extent, deviation, bound, shards=(), kind=jnp.bfloat16):
    array = deviation * jax.random.normal(own_key, extent, jnp.float32)
    if shards:
        array = array * level_of(own_key, extent, shards, -0.22, 0.18)
    return jnp.clip(array, -bound, bound).astype(kind)


def setup_inputs(seed: int = 0) -> dict:
    splits = jax.random.split(jax.random.key(seed), 10)
    features = centred(splits[0], (NODES, F), 1.0, 6.0, ((0, 1024),))
    weight = centred(splits[1], (F, F), F ** -0.5, 0.375)
    bias = centred(splits[2], (F,), 0.5, 3.0, (), jnp.float32)
    dense_adj = centred(splits[3], (N_ROW, N_REP, BAND, PANEL, RS), (BAND * PANEL + SPMAX * BLK) ** -0.5, 0.078125, ((0, 128), (1, 8)))
    dense_mask = with_ends((jax.random.randint(splits[4], (N_ROW, N_REP, BAND, PANEL // BLK, RS // BLK), 0, 4) < 3).astype(jnp.int32), jax.random.fold_in(splits[4], 1), 0, 1)
    sparse_adj = centred(splits[5], (N_ROW, N_REP, PANEL, SPMAX * BLK), (BAND * PANEL + SPMAX * BLK) ** -0.5, 0.078125, ((0, 128), (1, 8)))
    sparse_cols = with_ends(jax.random.randint(splits[6], (N_ROW, N_REP, SPMAX), 0, PANEL // BLK), jax.random.fold_in(splits[6], 1), 0, (PANEL // BLK) - 1).astype(jnp.int32)
    sparse_count = draw_sparse_count(jax.random.fold_in(splits[9], 71), 0)
    cotangent = centred(splits[8], (NODES, F), NODES ** -0.5, 0.015625, ((0, 1024),))
    return {"features": features, "weight": weight, "bias": bias, "dense_adj": dense_adj, "dense_mask": dense_mask, "sparse_adj": sparse_adj, "sparse_cols": sparse_cols, "sparse_count": sparse_count, "cotangent": cotangent}


def reference(features, weight, bias, dense_adj, dense_mask, sparse_adj, sparse_cols, sparse_count, cotangent):
    pieces = features.reshape(N_ROW, N_REP, RS, F)
    rows_tile = PANEL // BLK
    cols_tile = RS // BLK

    def partial_sum(row_index, rep_index):
        dense_tiles = dense_adj[row_index, rep_index].reshape(BAND, rows_tile, BLK, cols_tile, BLK)
        keep_mask = dense_mask[row_index, rep_index][:, :, None, :, None] > 0
        dense_tiles = jnp.where(keep_mask, dense_tiles, jnp.zeros_like(dense_tiles)).reshape(BAND, PANEL, RS)
        summed = jnp.zeros((PANEL, F), jnp.float32)
        for offset in range(BAND):
            source = pieces[(row_index + offset - H) % N_ROW, rep_index]
            summed = summed + jnp.dot(dense_tiles[offset], source, preferred_element_type=jnp.float32)
        whole_panel = pieces[row_index].reshape(PANEL // BLK, BLK, F)
        blocks = whole_panel[sparse_cols[row_index, rep_index]]
        live_slots = jnp.arange(SPMAX, dtype=jnp.int32) < sparse_count[row_index, rep_index]
        blocks = jnp.where(live_slots[:, None, None], blocks, jnp.zeros_like(blocks)).reshape(SPMAX * BLK, F)
        summed = summed + jnp.dot(sparse_adj[row_index, rep_index], blocks, preferred_element_type=jnp.float32)
        return summed.astype(jnp.bfloat16)

    def row_group(row_index):
        partials = lax.map(lambda rep_index: partial_sum(row_index, rep_index), jnp.arange(N_REP, dtype=jnp.int32))
        return jnp.sum(partials.astype(jnp.float32), axis=0).astype(jnp.bfloat16)

    aggregated = lax.map(row_group, jnp.arange(N_ROW, dtype=jnp.int32)).reshape(NODES, F)
    pre_act = jnp.dot(aggregated, weight, preferred_element_type=jnp.float32) + bias
    sigmoid_part = jax.nn.sigmoid(pre_act)
    activated = (pre_act * sigmoid_part).astype(jnp.bfloat16)
    slope = sigmoid_part * (1.0 + pre_act * (1.0 - sigmoid_part))
    grad_pre = (cotangent.astype(jnp.float32) * slope).astype(jnp.bfloat16)
    weight_grad = jnp.dot(aggregated.T, grad_pre, preferred_element_type=jnp.float32)
    bias_grad = jnp.sum(grad_pre.astype(jnp.float32), axis=0)
    return activated, weight_grad, bias_grad
```

```python
import jax
import jax.numpy as jnp
from jax import lax
from jax.experimental import pallas as pl
from jax.experimental.pallas import tpu as pltpu
from jax.sharding import Mesh, PartitionSpec as P

BLK = 128
ROW_STEP = 256
AXES = ("yh", "x", "z", "yl", "core")
SIZES = (2, 4, 16, 4, 2)
ROW = ("yh", "x", "z")
REP = ("yl", "core")
PLANE = ("yh", "x", "yl", "core")
DEPTH = "z"


def fetched_from(value, distance):
    count = lax.axis_size(ROW)
    return lax.ppermute(value, ROW, [(i, (i - distance) % count) for i in range(count)])


def partial_kernel(
    mask_ref, cols_ref, count_ref, f0, f1, f2, f3, f4, panel_ref, dense_ref, sparse_ref, out_ref, rhs
):
    step = pl.program_id(0)
    band = dense_ref.shape[0]
    slots = cols_ref.shape[0]

    @pl.when(step == 0)
    def _():
        for offset, ref in enumerate((f0, f1, f2, f3, f4)):
            rhs[offset * BLK : (offset + 1) * BLK, :] = ref[...]
        for slot in range(slots):
            at = (band + slot) * BLK
            block = panel_ref[cols_ref[slot]]
            rhs[at : at + BLK, :] = jnp.where(slot < count_ref[0], block, jnp.zeros_like(block))

    tiles = ROW_STEP // BLK
    lhs = []
    for offset in range(band):
        kept = []
        for tile in range(tiles):
            block = dense_ref[offset, tile * BLK : (tile + 1) * BLK, :]
            keep = mask_ref[offset, step * tiles + tile] > 0
            kept.append(jnp.where(keep, block, jnp.zeros_like(block)))
        lhs.append(jnp.concatenate(kept, axis=0))
    lhs.append(sparse_ref[...])
    out_ref[...] = jnp.dot(
        jnp.concatenate(lhs, axis=1), rhs[...], preferred_element_type=jnp.float32
    ).astype(out_ref.dtype)


def partial_sums(mask, cols, count, pieces, panel, dense, sparse):
    band, rows, width = dense.shape
    features = panel.shape[-1]
    whole = lambda shape: pl.BlockSpec(shape, lambda i: (0,) * len(shape))
    smem = pl.BlockSpec(memory_space=pltpu.SMEM)
    depth = band * width + sparse.shape[1]
    return pl.pallas_call(
        partial_kernel,
        grid=(rows // ROW_STEP,),
        out_shape=jax.ShapeDtypeStruct((rows, features), jnp.bfloat16),
        in_specs=[smem, smem, smem]
        + [whole(piece.shape) for piece in pieces]
        + [
            whole(panel.shape),
            pl.BlockSpec((band, ROW_STEP, width), lambda i: (0, i, 0)),
            pl.BlockSpec((ROW_STEP, sparse.shape[1]), lambda i: (i, 0)),
        ],
        out_specs=pl.BlockSpec((ROW_STEP, features), lambda i: (i, 0)),
        scratch_shapes=[pltpu.VMEM((depth, features), jnp.bfloat16)],
        compiler_params=pltpu.CompilerParams(vmem_limit_bytes=24 * 2**20),
        cost_estimate=pl.CostEstimate(
            flops=2 * rows * depth * features, bytes_accessed=2 * rows * depth, transcendentals=0
        ),
    )(mask, cols, count, *pieces, panel, dense, sparse)


def layer_kernel(parts_ref, weight_ref, bias_ref, cotangent_ref, out_ref, grad_ref):
    total = parts_ref[0].astype(jnp.float32)
    for share in range(1, parts_ref.shape[0]):
        total = total + parts_ref[share].astype(jnp.float32)
    aggregated = total.astype(jnp.bfloat16)
    pre_act = jnp.dot(aggregated, weight_ref[...], preferred_element_type=jnp.float32) + bias_ref[...]
    sigmoid_part = jax.nn.sigmoid(pre_act)
    out_ref[...] = (pre_act * sigmoid_part).astype(jnp.bfloat16)
    slope = sigmoid_part * (1.0 + pre_act * (1.0 - sigmoid_part))
    grad_pre = (cotangent_ref[...].astype(jnp.float32) * slope).astype(jnp.bfloat16)
    weight_grad = lax.dot_general(
        aggregated, grad_pre, (((0,), (0,)), ((), ())), preferred_element_type=jnp.float32
    )
    bias_grad = jnp.sum(grad_pre.astype(jnp.float32), axis=0, keepdims=True)
    halves, blocks = grad_ref.shape[0], grad_ref.shape[1]
    for half in range(halves):
        at = slice(half * BLK, (half + 1) * BLK)
        tile = weight_grad[:, at].reshape(blocks, 8, BLK)
        extra = jnp.broadcast_to(bias_grad[None, :, at], (blocks, 8, BLK))
        grad_ref[half] = jnp.concatenate([tile, extra], axis=1).astype(grad_ref.dtype)


def layer(parts, weight, bias, cotangent):
    rows, features = cotangent.shape
    return pl.pallas_call(
        layer_kernel,
        out_shape=(
            jax.ShapeDtypeStruct((rows, features), jnp.bfloat16),
            jax.ShapeDtypeStruct((features // BLK, features // 8, 16, BLK), jnp.bfloat16),
        ),
        compiler_params=pltpu.CompilerParams(vmem_limit_bytes=24 * 2**20),
    )(parts, weight, bias.reshape(1, features), cotangent)


def exchanged(pieces, axes):
    return lax.all_to_all(pieces, axes, 0, 0, tiled=False)


def spread(piece, axes):
    return exchanged(jnp.broadcast_to(piece[None], (lax.axis_size(axes),) + piece.shape), axes)


def summed(pieces):
    return jnp.sum(pieces.astype(jnp.float32), axis=0).astype(jnp.bfloat16)


def on_device(
    features, weight, bias, dense_adj, dense_mask, sparse_adj, sparse_cols, sparse_count, cotangent
):
    band, rows = dense_adj.shape[2], dense_adj.shape[3]
    reach = (band - 1) // 2
    width = features.shape[1]
    pieces = [
        features if offset == reach else fetched_from(features, offset - reach)
        for offset in range(band)
    ]
    panel = lax.all_gather(features, REP, axis=0, tiled=False)
    partial = partial_sums(
        dense_mask.reshape(band, rows // BLK),
        sparse_cols.reshape(-1),
        sparse_count.reshape(-1),
        pieces,
        panel,
        dense_adj[0, 0],
        sparse_adj[0, 0],
    )
    shares = lax.axis_size(REP)
    parts = exchanged(partial.reshape(shares, rows // shares, width), REP)
    activated, grads = layer(parts, weight, bias, cotangent)
    halves, blocks = grads.shape[:2]
    mine = summed(exchanged(grads.reshape((halves * blocks,) + grads.shape[2:]), PLANE))
    mine = summed(spread(mine, DEPTH))
    grads = spread(mine, PLANE).reshape(grads.shape).astype(jnp.float32)
    weight_grad = grads[:, :, :8].transpose(1, 2, 0, 3).reshape(width, width)
    bias_grad = grads[:, 0, 8].reshape(width)
    return activated, weight_grad, bias_grad


def solution(mesh):
    fine = Mesh(mesh.devices.reshape(SIZES), AXES)
    nodes = P(AXES, None)
    in_specs = (
        nodes,
        P(),
        P(),
        P(ROW, REP, None, None, None),
        P(ROW, REP, None, None, None),
        P(ROW, REP, None, None),
        P(ROW, REP, None),
        P(ROW, REP),
        nodes,
    )
    return jax.shard_map(
        on_device, mesh=fine, in_specs=in_specs, out_specs=(nodes, P(), P()), check_vma=False
    )
```

```python
import jax
import jax.numpy as jnp
from jax import lax
from jax.experimental import pallas as pl
from jax.experimental.pallas import tpu as pltpu
from jax.sharding import Mesh, PartitionSpec as P

BLK = 128
ROW_STEP = 256
AXES = ("yh", "x", "z", "yl", "core")
SIZES = (2, 4, 16, 4, 2)
ROW = ("yh", "x", "z")
REP = ("yl", "core")
PLANE = ("yh", "x", "yl", "core")
DEPTH = "z"
SMALL = pltpu.CompilerParams(vmem_limit_bytes=8 * 2**20)


def fetched_from(value, distance):
    count = lax.axis_size(ROW)
    return lax.ppermute(value, ROW, [(i, (i - distance) % count) for i in range(count)])


def partial_kernel(
    mask_hbm, cols_hbm, count_hbm, f3, f1, f0, f4, panel_ref, dense_hbm, sparse_hbm, out_ref,
    mask, cols, count, dense, sparse, rhs, small_sems, dense_sems, sparse_sems,
):
    band, rows = dense.shape[:2]
    slots = cols.shape[-1]
    steps = rows // ROW_STEP
    small = [
        pltpu.make_async_copy(source, target, small_sems.at[i])
        for i, (source, target) in enumerate(
            ((cols_hbm, cols), (count_hbm, count), (mask_hbm, mask))
        )
    ]
    large = []
    for step in range(steps):
        at = pl.ds(step * ROW_STEP, ROW_STEP)
        large.append(
            (
                pltpu.make_async_copy(dense_hbm.at[:, at, :], dense.at[:, at, :], dense_sems.at[step]),
                pltpu.make_async_copy(sparse_hbm.at[at, :], sparse.at[at, :], sparse_sems.at[step]),
            )
        )
    for copy in small:
        copy.start()
    for pair in large:
        for copy in pair:
            copy.start()
    share = lax.axis_index("yl") * lax.axis_size("core") + lax.axis_index("core")
    for offset, ref in enumerate((f0, f1, panel_ref.at[share], f3, f4)):
        rhs[offset * BLK : (offset + 1) * BLK, :] = ref[...]
    for copy in small:
        copy.wait()
    for slot in range(slots):
        at = (band + slot) * BLK
        block = panel_ref[cols[0, 0, slot]]
        live = slot < count[0, 0]
        rhs[at : at + BLK, :] = jnp.where(live, block, jnp.zeros_like(block))
    tiles = ROW_STEP // BLK
    for step in range(steps):
        for copy in large[step]:
            copy.wait()
        lhs = []
        for offset in range(band):
            kept = []
            for tile in range(step * tiles, (step + 1) * tiles):
                block = dense[offset, tile * BLK : (tile + 1) * BLK, :]
                kept.append(jnp.where(mask[offset, 0, tile] > 0, block, jnp.zeros_like(block)))
            lhs.append(jnp.concatenate(kept, axis=0))
        at = slice(step * ROW_STEP, (step + 1) * ROW_STEP)
        lhs.append(sparse[at, :])
        out_ref[at, :] = jnp.dot(
            jnp.concatenate(lhs, axis=1), rhs[...], preferred_element_type=jnp.float32
        ).astype(out_ref.dtype)


def partial_sums(mask, cols, count, neighbours, panel, dense, sparse):
    band, rows, width = dense.shape
    features = panel.shape[-1]
    hbm = pl.BlockSpec(memory_space=pltpu.HBM)
    vmem = pl.BlockSpec(memory_space=pltpu.VMEM)
    depth = band * width + sparse.shape[1]
    steps = rows // ROW_STEP
    return pl.pallas_call(
        partial_kernel,
        out_shape=jax.ShapeDtypeStruct((rows, features), jnp.bfloat16),
        in_specs=[hbm] * 3 + [vmem] * 5 + [hbm] * 2,
        out_specs=vmem,
        scratch_shapes=[
            pltpu.SMEM(mask.shape, jnp.int32),
            pltpu.SMEM(cols.shape, jnp.int32),
            pltpu.SMEM(count.shape, jnp.int32),
            pltpu.VMEM(dense.shape, jnp.bfloat16),
            pltpu.VMEM(sparse.shape, jnp.bfloat16),
            pltpu.VMEM((depth, features), jnp.bfloat16),
            pltpu.SemaphoreType.DMA((3,)),
            pltpu.SemaphoreType.DMA((steps,)),
            pltpu.SemaphoreType.DMA((steps,)),
        ],
        compiler_params=pltpu.CompilerParams(vmem_limit_bytes=52 * 2**20),
        cost_estimate=pl.CostEstimate(
            flops=2 * rows * depth * features, bytes_accessed=2 * rows * depth, transcendentals=0
        ),
    )(mask, cols, count, *neighbours, panel, dense, sparse)


def layer_kernel(parts_ref, weight_ref, bias_ref, cotangent_ref, out_ref, grad_ref):
    aggregated = total_of(parts_ref).astype(jnp.bfloat16)
    pre_act = jnp.dot(aggregated, weight_ref[...], preferred_element_type=jnp.float32) + bias_ref[...]
    sigmoid_part = jax.nn.sigmoid(pre_act)
    out_ref[...] = (pre_act * sigmoid_part).astype(jnp.bfloat16)
    slope = sigmoid_part * (1.0 + pre_act * (1.0 - sigmoid_part))
    grad_pre = (cotangent_ref[...].astype(jnp.float32) * slope).astype(jnp.bfloat16)
    weight_grad = lax.dot_general(
        aggregated, grad_pre, (((0,), (0,)), ((), ())), preferred_element_type=jnp.float32
    )
    bias_grad = jnp.sum(grad_pre.astype(jnp.float32), axis=0, keepdims=True)
    halves, blocks = grad_ref.shape[0], grad_ref.shape[1]
    lines = [bias_grad[:, half * BLK : (half + 1) * BLK] for half in range(halves)]
    lines.append(jnp.zeros((8 - halves, BLK), jnp.float32))
    extra = jnp.broadcast_to(jnp.concatenate(lines, axis=0)[None], (blocks, 8, BLK))
    for half in range(halves):
        tile = weight_grad[:, half * BLK : (half + 1) * BLK].reshape(blocks, 8, BLK)
        grad_ref[half] = jnp.concatenate([tile, extra], axis=1).astype(grad_ref.dtype)


def layer(parts, weight, bias, cotangent):
    rows, features = cotangent.shape
    return pl.pallas_call(
        layer_kernel,
        out_shape=(
            jax.ShapeDtypeStruct((rows, features), jnp.bfloat16),
            jax.ShapeDtypeStruct((features // BLK, features // 8, 16, BLK), jnp.bfloat16),
        ),
        compiler_params=pltpu.CompilerParams(vmem_limit_bytes=16 * 2**20),
    )(parts, weight, bias.reshape(1, features), cotangent)


def total_of(parts_ref):
    total = parts_ref[0].astype(jnp.float32)
    for part in range(1, parts_ref.shape[0]):
        total = total + parts_ref[part].astype(jnp.float32)
    return total


def plane_kernel(parts_ref, out_ref):
    total = total_of(parts_ref).astype(out_ref.dtype)
    out_ref[...] = jnp.broadcast_to(total[None], out_ref.shape)


def depth_kernel(parts_ref, out_ref, bias_ref):
    total = total_of(parts_ref)
    halves = bias_ref.shape[1] // BLK
    bias_ref[...] = jnp.concatenate([total[8 + half : 9 + half] for half in range(halves)], axis=1)
    out_ref[...] = jnp.broadcast_to(total[:8].astype(out_ref.dtype)[None], out_ref.shape)


def unpack_kernel(pieces_ref, out_ref):
    for half in range(pieces_ref.shape[0]):
        tile = pieces_ref[half].astype(jnp.float32)
        out_ref[:, half * BLK : (half + 1) * BLK] = tile.reshape(out_ref.shape[0], BLK)


def exchanged(pieces, axes):
    return lax.all_to_all(pieces, axes, 0, 0, tiled=False)


def summed_over_devices(grads):
    halves, blocks, rows, _ = grads.shape
    features = halves * BLK
    plane, depth = lax.axis_size(PLANE), lax.axis_size(DEPTH)
    mine = pl.pallas_call(
        plane_kernel, out_shape=jax.ShapeDtypeStruct((depth, rows, BLK), jnp.bfloat16), compiler_params=SMALL
    )(exchanged(grads.reshape(plane, rows, BLK), PLANE))
    mine, bias_grad = pl.pallas_call(
        depth_kernel,
        out_shape=(
            jax.ShapeDtypeStruct((plane, 8, BLK), jnp.bfloat16),
            jax.ShapeDtypeStruct((1, features), jnp.float32),
        ),
        compiler_params=SMALL,
    )(exchanged(mine, DEPTH))
    weight_grad = pl.pallas_call(
        unpack_kernel,
        out_shape=jax.ShapeDtypeStruct((blocks * 8, features), jnp.float32),
        compiler_params=SMALL,
    )(exchanged(mine, PLANE).reshape(halves, blocks, 8, BLK))
    return weight_grad, bias_grad.reshape(features)


def on_device(
    features, weight, bias, dense_adj, dense_mask, sparse_adj, sparse_cols, sparse_count, cotangent
):
    band, rows = dense_adj.shape[2], dense_adj.shape[3]
    reach = (band - 1) // 2
    width = features.shape[1]
    neighbours = [fetched_from(features, k) for k in (1, -1, -2, 2)]
    panel = lax.all_gather(features, REP, axis=0, tiled=False)
    partial = partial_sums(
        dense_mask.reshape(band, 1, rows // BLK),
        sparse_cols,
        sparse_count,
        neighbours,
        panel,
        dense_adj[0, 0],
        sparse_adj[0, 0],
    )
    shares = lax.axis_size(REP)
    parts = exchanged(partial.reshape(shares, rows // shares, width), REP)
    activated, grads = layer(parts, weight, bias, cotangent)
    weight_grad, bias_grad = summed_over_devices(grads)
    return activated, weight_grad, bias_grad


def solution(mesh):
    fine = Mesh(mesh.devices.reshape(SIZES), AXES)
    nodes = P(AXES, None)
    in_specs = (
        nodes,
        P(),
        P(),
        P(ROW, REP, None, None, None),
        P(ROW, REP, None, None, None),
        P(ROW, REP, None, None),
        P(ROW, REP, None),
        P(ROW, REP),
        nodes,
    )
    return jax.shard_map(
        on_device, mesh=fine, in_specs=in_specs, out_specs=(nodes, P(), P()), check_vma=False
    )
```

```python
import jax
import jax.numpy as jnp
from jax import lax
from jax.experimental import pallas as pl
from jax.experimental.pallas import tpu as pltpu
from jax.sharding import Mesh, PartitionSpec as P

BLK = 128
ROW_STEP = 256
AXES = ("yh", "x", "z", "yl", "core")
SIZES = (2, 4, 16, 4, 2)
ROW = ("yh", "x", "z")
REP = ("yl", "core")
PLANE = ("yh", "x", "yl", "core")
DEPTH = "z"
SMALL = pltpu.CompilerParams(vmem_limit_bytes=8 * 2**20)


def fetched_from(value, distance):
    count = lax.axis_size(ROW)
    return lax.ppermute(value, ROW, [(i, (i - distance) % count) for i in range(count)])


def partial_kernel(
    mask_hbm, cols_hbm, count_hbm, f3, f1, f0, f4, panel_ref, dense_hbm, sparse_hbm, out_ref,
    mask, cols, count, dense, sparse, rhs, small_sems, dense_sems, sparse_sems,
):
    band, rows = dense.shape[:2]
    slots = cols.shape[-1]
    steps = rows // ROW_STEP
    small = [
        pltpu.make_async_copy(source, target, small_sems.at[i])
        for i, (source, target) in enumerate(
            ((cols_hbm, cols), (count_hbm, count), (mask_hbm, mask))
        )
    ]
    large = []
    for step in range(steps):
        at = pl.ds(step * ROW_STEP, ROW_STEP)
        large.append(
            (
                pltpu.make_async_copy(dense_hbm.at[:, at, :], dense.at[:, at, :], dense_sems.at[step]),
                pltpu.make_async_copy(sparse_hbm.at[at, :], sparse.at[at, :], sparse_sems.at[step]),
            )
        )
    for copy in small:
        copy.start()
    for pair in large:
        for copy in pair:
            copy.start()
    share = lax.axis_index("yl") * lax.axis_size("core") + lax.axis_index("core")
    for offset, ref in enumerate((f0, f1, panel_ref.at[share], f3, f4)):
        rhs[offset * BLK : (offset + 1) * BLK, :] = ref[...]
    for copy in small:
        copy.wait()
    for slot in range(slots):
        at = (band + slot) * BLK
        block = panel_ref[cols[0, 0, slot]]
        live = slot < count[0, 0]
        rhs[at : at + BLK, :] = jnp.where(live, block, jnp.zeros_like(block))
    tiles = ROW_STEP // BLK
    for step in range(steps):
        for copy in large[step]:
            copy.wait()
        lhs = []
        for offset in range(band):
            kept = []
            for tile in range(step * tiles, (step + 1) * tiles):
                block = dense[offset, tile * BLK : (tile + 1) * BLK, :]
                kept.append(jnp.where(mask[offset, 0, tile] > 0, block, jnp.zeros_like(block)))
            lhs.append(jnp.concatenate(kept, axis=0))
        at = slice(step * ROW_STEP, (step + 1) * ROW_STEP)
        lhs.append(sparse[at, :])
        out_ref[at, :] = jnp.dot(
            jnp.concatenate(lhs, axis=1), rhs[...], preferred_element_type=jnp.float32
        ).astype(out_ref.dtype)


def partial_sums(mask, cols, count, neighbours, panel, dense, sparse):
    band, rows, width = dense.shape
    features = panel.shape[-1]
    hbm = pl.BlockSpec(memory_space=pltpu.HBM)
    vmem = pl.BlockSpec(memory_space=pltpu.VMEM)
    depth = band * width + sparse.shape[1]
    steps = rows // ROW_STEP
    return pl.pallas_call(
        partial_kernel,
        out_shape=jax.ShapeDtypeStruct((rows, features), jnp.bfloat16),
        in_specs=[hbm] * 3 + [vmem] * 5 + [hbm] * 2,
        out_specs=vmem,
        scratch_shapes=[
            pltpu.SMEM(mask.shape, jnp.int32),
            pltpu.SMEM(cols.shape, jnp.int32),
            pltpu.SMEM(count.shape, jnp.int32),
            pltpu.VMEM(dense.shape, jnp.bfloat16),
            pltpu.VMEM(sparse.shape, jnp.bfloat16),
            pltpu.VMEM((depth, features), jnp.bfloat16),
            pltpu.SemaphoreType.DMA((3,)),
            pltpu.SemaphoreType.DMA((steps,)),
            pltpu.SemaphoreType.DMA((steps,)),
        ],
        compiler_params=pltpu.CompilerParams(vmem_limit_bytes=52 * 2**20),
        cost_estimate=pl.CostEstimate(
            flops=2 * rows * depth * features, bytes_accessed=2 * rows * depth, transcendentals=0
        ),
    )(mask, cols, count, *neighbours, panel, dense, sparse)


def layer_kernel(parts_ref, weight_ref, bias_ref, cotangent_ref, out_ref, grad_ref):
    aggregated = total_of(parts_ref).astype(jnp.bfloat16)
    pre_act = jnp.dot(aggregated, weight_ref[...], preferred_element_type=jnp.float32) + bias_ref[...]
    sigmoid_part = jax.nn.sigmoid(pre_act)
    out_ref[...] = (pre_act * sigmoid_part).astype(jnp.bfloat16)
    slope = sigmoid_part * (1.0 + pre_act * (1.0 - sigmoid_part))
    grad_pre = (cotangent_ref[...].astype(jnp.float32) * slope).astype(jnp.bfloat16)
    weight_grad = lax.dot_general(
        aggregated, grad_pre, (((0,), (0,)), ((), ())), preferred_element_type=jnp.float32
    )
    bias_grad = jnp.sum(grad_pre.astype(jnp.float32), axis=0, keepdims=True)
    halves = bias_grad.shape[1] // BLK
    blocks = grad_ref.shape[0] // halves
    extra = jnp.concatenate([bias_grad[:, h * BLK : (h + 1) * BLK] for h in range(halves)], axis=0)
    extra = jnp.broadcast_to(extra[None], (blocks,) + extra.shape).astype(grad_ref.dtype)
    for half in range(halves):
        tile = weight_grad[:, half * BLK : (half + 1) * BLK].reshape(blocks, 8, BLK)
        at = slice(half * blocks, (half + 1) * blocks)
        for pair in range(4):
            lanes = slice(pair * BLK, (pair + 1) * BLK)
            grad_ref[at, :, lanes] = tile[:, 2 * pair : 2 * pair + 2, :].astype(grad_ref.dtype)
        grad_ref[at, :, 4 * BLK :] = extra


def layer(parts, weight, bias, cotangent):
    rows, features = cotangent.shape
    return pl.pallas_call(
        layer_kernel,
        out_shape=(
            jax.ShapeDtypeStruct((rows, features), jnp.bfloat16),
            jax.ShapeDtypeStruct((features // BLK * features // 8, 2, 5 * BLK), jnp.bfloat16),
        ),
        compiler_params=pltpu.CompilerParams(vmem_limit_bytes=16 * 2**20),
    )(parts, weight, bias.reshape(1, features), cotangent)


def total_of(parts_ref):
    total = parts_ref[0].astype(jnp.float32)
    for part in range(1, parts_ref.shape[0]):
        total = total + parts_ref[part].astype(jnp.float32)
    return total


def plane_kernel(parts_ref, out_ref):
    total = total_of(parts_ref)
    lines = [total[:, at : at + BLK] for at in range(0, total.shape[1], BLK)]
    lines.append(jnp.zeros((6, BLK), jnp.float32))
    total = jnp.concatenate(lines, axis=0).astype(out_ref.dtype)
    out_ref[...] = jnp.broadcast_to(total[None], out_ref.shape)


def depth_kernel(parts_ref, out_ref, bias_ref):
    total = total_of(parts_ref)
    halves = bias_ref.shape[1] // BLK
    bias_ref[...] = jnp.concatenate([total[8 + half : 9 + half] for half in range(halves)], axis=1)
    out_ref[...] = jnp.broadcast_to(total[:8].astype(out_ref.dtype)[None], out_ref.shape)


def unpack_kernel(pieces_ref, out_ref):
    for half in range(pieces_ref.shape[0]):
        tile = pieces_ref[half].astype(jnp.float32)
        out_ref[:, half * BLK : (half + 1) * BLK] = tile.reshape(out_ref.shape[0], BLK)


def exchanged(pieces, axes):
    return lax.all_to_all(pieces, axes, 0, 0, tiled=False)


def summed_over_devices(grads):
    plane, depth = lax.axis_size(PLANE), lax.axis_size(DEPTH)
    halves = 2
    blocks, features = grads.shape[0] // halves, halves * BLK
    mine = pl.pallas_call(
        plane_kernel, out_shape=jax.ShapeDtypeStruct((depth, 16, BLK), jnp.bfloat16), compiler_params=SMALL
    )(exchanged(grads, PLANE))
    mine, bias_grad = pl.pallas_call(
        depth_kernel,
        out_shape=(
            jax.ShapeDtypeStruct((plane, 8, BLK), jnp.bfloat16),
            jax.ShapeDtypeStruct((1, features), jnp.float32),
        ),
        compiler_params=SMALL,
    )(exchanged(mine, DEPTH))
    weight_grad = pl.pallas_call(
        unpack_kernel,
        out_shape=jax.ShapeDtypeStruct((blocks * 8, features), jnp.float32),
        compiler_params=SMALL,
    )(exchanged(mine, PLANE).reshape(halves, blocks, 8, BLK))
    return weight_grad, bias_grad.reshape(features)


def on_device(
    features, weight, bias, dense_adj, dense_mask, sparse_adj, sparse_cols, sparse_count, cotangent
):
    band, rows = dense_adj.shape[2], dense_adj.shape[3]
    reach = (band - 1) // 2
    width = features.shape[1]
    neighbours = [fetched_from(features, k) for k in (1, -1, -2, 2)]
    panel = lax.all_gather(features, REP, axis=0, tiled=False)
    partial = partial_sums(
        dense_mask.reshape(band, 1, rows // BLK),
        sparse_cols,
        sparse_count,
        neighbours,
        panel,
        dense_adj[0, 0],
        sparse_adj[0, 0],
    )
    shares = lax.axis_size(REP)
    parts = exchanged(partial.reshape(shares, rows // shares, width), REP)
    activated, grads = layer(parts, weight, bias, cotangent)
    weight_grad, bias_grad = summed_over_devices(grads)
    return activated, weight_grad, bias_grad


def solution(mesh):
    fine = Mesh(mesh.devices.reshape(SIZES), AXES)
    nodes = P(AXES, None)
    in_specs = (
        nodes,
        P(),
        P(),
        P(ROW, REP, None, None, None),
        P(ROW, REP, None, None, None),
        P(ROW, REP, None, None),
        P(ROW, REP, None),
        P(ROW, REP),
        nodes,
    )
    return jax.shard_map(
        on_device, mesh=fine, in_specs=in_specs, out_specs=(nodes, P(), P()), check_vma=False
    )
```

```python
import jax
import jax.numpy as jnp
from jax import lax
from jax.experimental import pallas as pl
from jax.experimental.pallas import tpu as pltpu
from jax.sharding import Mesh, PartitionSpec as P

BLK = 128
ROW_STEP = 256
AXES = ("yh", "x", "z", "yl", "core")
SIZES = (2, 4, 16, 4, 2)
ROW = ("yh", "x", "z")
REP = ("yl", "core")
PLANE = ("yh", "x", "yl", "core")
DEPTH = "z"
SMALL = pltpu.CompilerParams(vmem_limit_bytes=8 * 2**20)


def fetched_from(value, distance):
    count = lax.axis_size(ROW)
    return lax.ppermute(value, ROW, [(i, (i - distance) % count) for i in range(count)])


def partial_kernel(
    mask_hbm, cols_hbm, count_hbm, f3, f1, f0, f4, panel_ref, dense_hbm, sparse_hbm, out_ref,
    mask, cols, count, dense, sparse, rhs, small_sems, dense_sems, sparse_sems,
):
    band, rows = dense.shape[:2]
    slots = cols.shape[-1]
    steps = rows // ROW_STEP
    small = [
        pltpu.make_async_copy(source, target, small_sems.at[i])
        for i, (source, target) in enumerate(
            ((cols_hbm, cols), (count_hbm, count), (mask_hbm, mask))
        )
    ]
    large = []
    for step in range(steps):
        at = pl.ds(step * ROW_STEP, ROW_STEP)
        large.append(
            (
                pltpu.make_async_copy(dense_hbm.at[:, at, :], dense.at[:, at, :], dense_sems.at[step]),
                pltpu.make_async_copy(sparse_hbm.at[at, :], sparse.at[at, :], sparse_sems.at[step]),
            )
        )
    for copy in small:
        copy.start()
    for pair in large:
        for copy in pair:
            copy.start()
    share = lax.axis_index("yl") * lax.axis_size("core") + lax.axis_index("core")
    for offset, ref in enumerate((f0, f1, panel_ref.at[share], f3, f4)):
        rhs[offset * BLK : (offset + 1) * BLK, :] = ref[...]
    for copy in small:
        copy.wait()
    for slot in range(slots):
        at = (band + slot) * BLK
        block = panel_ref[cols[0, 0, slot]]
        live = slot < count[0, 0]
        rhs[at : at + BLK, :] = jnp.where(live, block, jnp.zeros_like(block))
    tiles = ROW_STEP // BLK
    for step in range(steps):
        for copy in large[step]:
            copy.wait()
        lhs = []
        for offset in range(band):
            kept = []
            for tile in range(step * tiles, (step + 1) * tiles):
                block = dense[offset, tile * BLK : (tile + 1) * BLK, :]
                kept.append(jnp.where(mask[offset, 0, tile] > 0, block, jnp.zeros_like(block)))
            lhs.append(jnp.concatenate(kept, axis=0))
        at = slice(step * ROW_STEP, (step + 1) * ROW_STEP)
        lhs.append(sparse[at, :])
        out_ref[at, :] = jnp.dot(
            jnp.concatenate(lhs, axis=1), rhs[...], preferred_element_type=jnp.float32
        ).astype(out_ref.dtype)


def partial_sums(mask, cols, count, neighbours, panel, dense, sparse):
    band, rows, width = dense.shape
    features = panel.shape[-1]
    hbm = pl.BlockSpec(memory_space=pltpu.HBM)
    vmem = pl.BlockSpec(memory_space=pltpu.VMEM)
    depth = band * width + sparse.shape[1]
    steps = rows // ROW_STEP
    return pl.pallas_call(
        partial_kernel,
        out_shape=jax.ShapeDtypeStruct((rows, features), jnp.bfloat16),
        in_specs=[hbm] * 3 + [vmem] * 5 + [hbm] * 2,
        out_specs=vmem,
        scratch_shapes=[
            pltpu.SMEM(mask.shape, jnp.int32),
            pltpu.SMEM(cols.shape, jnp.int32),
            pltpu.SMEM(count.shape, jnp.int32),
            pltpu.VMEM(dense.shape, jnp.bfloat16),
            pltpu.VMEM(sparse.shape, jnp.bfloat16),
            pltpu.VMEM((depth, features), jnp.bfloat16),
            pltpu.SemaphoreType.DMA((3,)),
            pltpu.SemaphoreType.DMA((steps,)),
            pltpu.SemaphoreType.DMA((steps,)),
        ],
        compiler_params=pltpu.CompilerParams(vmem_limit_bytes=52 * 2**20),
        cost_estimate=pl.CostEstimate(
            flops=2 * rows * depth * features, bytes_accessed=2 * rows * depth, transcendentals=0
        ),
    )(mask, cols, count, *neighbours, panel, dense, sparse)


def layer_kernel(parts_ref, weight_ref, bias_ref, cotangent_ref, out_ref, grad_ref):
    aggregated = total_of(parts_ref).astype(jnp.bfloat16)
    pre_act = jnp.dot(aggregated, weight_ref[...], preferred_element_type=jnp.float32) + bias_ref[...]
    sigmoid_part = jax.nn.sigmoid(pre_act)
    out_ref[...] = (pre_act * sigmoid_part).astype(jnp.bfloat16)
    slope = sigmoid_part * (1.0 + pre_act * (1.0 - sigmoid_part))
    grad_pre = (cotangent_ref[...].astype(jnp.float32) * slope).astype(jnp.bfloat16)
    weight_grad = lax.dot_general(
        aggregated, grad_pre, (((0,), (0,)), ((), ())), preferred_element_type=jnp.float32
    )
    bias_grad = jnp.sum(grad_pre.astype(jnp.float32), axis=0, keepdims=True)
    halves = bias_grad.shape[1] // BLK
    blocks = grad_ref.shape[0] // halves
    extra = jnp.concatenate([bias_grad[:, h * BLK : (h + 1) * BLK] for h in range(halves)], axis=0)
    extra = jnp.broadcast_to(extra[None], (blocks,) + extra.shape).astype(grad_ref.dtype)
    for half in range(halves):
        tile = weight_grad[:, half * BLK : (half + 1) * BLK].reshape(blocks, 8, BLK)
        at = slice(half * blocks, (half + 1) * blocks)
        for pair in range(4):
            lanes = slice(pair * BLK, (pair + 1) * BLK)
            grad_ref[at, :, lanes] = tile[:, 2 * pair : 2 * pair + 2, :].astype(grad_ref.dtype)
        grad_ref[at, :, 4 * BLK :] = extra


def layer(parts, weight, bias, cotangent):
    rows, features = cotangent.shape
    return pl.pallas_call(
        layer_kernel,
        out_shape=(
            jax.ShapeDtypeStruct((rows, features), jnp.bfloat16),
            jax.ShapeDtypeStruct((features // BLK * features // 8, 2, 5 * BLK), jnp.bfloat16),
        ),
        compiler_params=pltpu.CompilerParams(vmem_limit_bytes=16 * 2**20),
    )(parts, weight, bias.reshape(1, features), cotangent)


def total_of(parts_ref):
    total = parts_ref[0].astype(jnp.float32)
    for part in range(1, parts_ref.shape[0]):
        total = total + parts_ref[part].astype(jnp.float32)
    return total


def plane_kernel(parts_ref, out_ref):
    total = total_of(parts_ref).astype(out_ref.dtype)
    out_ref[...] = jnp.broadcast_to(total[None], out_ref.shape)


def depth_kernel(parts_ref, out_ref, bias_ref):
    total = total_of(parts_ref)
    pairs = out_ref.shape[1] // 2
    bias = total[:, pairs * BLK :]
    bias_ref[...] = jnp.concatenate([bias[half : half + 1] for half in range(bias.shape[0])], axis=1)
    tile = jnp.concatenate([total[:, pair * BLK : (pair + 1) * BLK] for pair in range(pairs)], axis=0)
    out_ref[...] = jnp.broadcast_to(tile.astype(out_ref.dtype)[None], out_ref.shape)


def unpack_kernel(pieces_ref, out_ref):
    for half in range(pieces_ref.shape[0]):
        tile = pieces_ref[half].astype(jnp.float32)
        out_ref[:, half * BLK : (half + 1) * BLK] = tile.reshape(out_ref.shape[0], BLK)


def exchanged(pieces, axes):
    return lax.all_to_all(pieces, axes, 0, 0, tiled=False)


def summed_over_devices(grads):
    plane, depth = lax.axis_size(PLANE), lax.axis_size(DEPTH)
    halves = 2
    blocks, features = grads.shape[0] // halves, halves * BLK
    mine = pl.pallas_call(
        plane_kernel, out_shape=jax.ShapeDtypeStruct((depth,) + grads.shape[1:], jnp.bfloat16), compiler_params=SMALL
    )(exchanged(grads, PLANE))
    mine, bias_grad = pl.pallas_call(
        depth_kernel,
        out_shape=(
            jax.ShapeDtypeStruct((plane, 8, BLK), jnp.bfloat16),
            jax.ShapeDtypeStruct((1, features), jnp.float32),
        ),
        compiler_params=SMALL,
    )(exchanged(mine, DEPTH))
    weight_grad = pl.pallas_call(
        unpack_kernel,
        out_shape=jax.ShapeDtypeStruct((blocks * 8, features), jnp.float32),
        compiler_params=SMALL,
    )(exchanged(mine, PLANE).reshape(halves, blocks, 8, BLK))
    return weight_grad, bias_grad.reshape(features)


def on_device(
    features, weight, bias, dense_adj, dense_mask, sparse_adj, sparse_cols, sparse_count, cotangent
):
    band, rows = dense_adj.shape[2], dense_adj.shape[3]
    reach = (band - 1) // 2
    width = features.shape[1]
    neighbours = [fetched_from(features, k) for k in (1, -1, -2, 2)]
    panel = lax.all_gather(features, REP, axis=0, tiled=False)
    partial = partial_sums(
        dense_mask.reshape(band, 1, rows // BLK),
        sparse_cols,
        sparse_count,
        neighbours,
        panel,
        dense_adj[0, 0],
        sparse_adj[0, 0],
    )
    shares = lax.axis_size(REP)
    parts = exchanged(partial.reshape(shares, rows // shares, width), REP)
    activated, grads = layer(parts, weight, bias, cotangent)
    weight_grad, bias_grad = summed_over_devices(grads)
    return activated, weight_grad, bias_grad


def solution(mesh):
    fine = Mesh(mesh.devices.reshape(SIZES), AXES)
    nodes = P(AXES, None)
    in_specs = (
        nodes,
        P(),
        P(),
        P(ROW, REP, None, None, None),
        P(ROW, REP, None, None, None),
        P(ROW, REP, None, None),
        P(ROW, REP, None),
        P(ROW, REP),
        nodes,
    )
    return jax.shard_map(
        on_device, mesh=fine, in_specs=in_specs, out_specs=(nodes, P(), P()), check_vma=False
    )
```

```python
import jax
import jax.numpy as jnp
from jax import lax
from jax.experimental import pallas as pl
from jax.experimental.pallas import tpu as pltpu
from jax.sharding import Mesh, PartitionSpec as P

BLK = 128
ROW_STEP = 512
AXES = ("yh", "x", "z", "yl", "core")
SIZES = (2, 4, 16, 4, 2)
ROW = ("yh", "x", "z")
REP = ("yl", "core")
PLANE = ("yh", "x", "yl", "core")
DEPTH = "z"
SMALL = pltpu.CompilerParams(vmem_limit_bytes=8 * 2**20)


def fetched_from(value, distance):
    count = lax.axis_size(ROW)
    return lax.ppermute(value, ROW, [(i, (i - distance) % count) for i in range(count)])


def partial_kernel(
    mask_hbm, cols_hbm, count_hbm, f3, f1, f0, f4, panel_ref, dense_hbm, sparse_hbm, out_ref,
    mask, cols, count, dense, sparse, rhs, small_sems, dense_sems, sparse_sems,
):
    band, rows = dense.shape[:2]
    slots = cols.shape[-1]
    steps = rows // ROW_STEP
    small = [
        pltpu.make_async_copy(source, target, small_sems.at[i])
        for i, (source, target) in enumerate(
            ((cols_hbm, cols), (count_hbm, count), (mask_hbm, mask))
        )
    ]
    large = []
    for step in range(steps):
        at = pl.ds(step * ROW_STEP, ROW_STEP)
        large.append(
            (
                pltpu.make_async_copy(dense_hbm.at[:, at, :], dense.at[:, at, :], dense_sems.at[step]),
                pltpu.make_async_copy(sparse_hbm.at[at, :], sparse.at[at, :], sparse_sems.at[step]),
            )
        )
    for copy in large[0]:
        copy.start()
    for copy in small:
        copy.start()
    for pair in large[1:]:
        for copy in pair:
            copy.start()
    share = lax.axis_index("yl") * lax.axis_size("core") + lax.axis_index("core")
    for offset, ref in enumerate((f0, f1, panel_ref.at[share], f3, f4)):
        rhs[offset * BLK : (offset + 1) * BLK, :] = ref[...]
    for copy in small:
        copy.wait()
    for slot in range(slots):
        at = (band + slot) * BLK
        block = panel_ref[cols[0, 0, slot]]
        live = slot < count[0, 0]
        rhs[at : at + BLK, :] = jnp.where(live, block, jnp.zeros_like(block))
    tiles = ROW_STEP // BLK
    for step in range(steps):
        for copy in large[step]:
            copy.wait()
        lhs = []
        for offset in range(band):
            kept = []
            for tile in range(step * tiles, (step + 1) * tiles):
                block = dense[offset, tile * BLK : (tile + 1) * BLK, :]
                kept.append(jnp.where(mask[offset, 0, tile] > 0, block, jnp.zeros_like(block)))
            lhs.append(jnp.concatenate(kept, axis=0))
        at = slice(step * ROW_STEP, (step + 1) * ROW_STEP)
        lhs.append(sparse[at, :])
        out_ref[at, :] = jnp.dot(
            jnp.concatenate(lhs, axis=1), rhs[...], preferred_element_type=jnp.float32
        ).astype(out_ref.dtype)


def partial_sums(mask, cols, count, neighbours, panel, dense, sparse):
    band, rows, width = dense.shape
    features = panel.shape[-1]
    hbm = pl.BlockSpec(memory_space=pltpu.HBM)
    vmem = pl.BlockSpec(memory_space=pltpu.VMEM)
    depth = band * width + sparse.shape[1]
    steps = rows // ROW_STEP
    return pl.pallas_call(
        partial_kernel,
        out_shape=jax.ShapeDtypeStruct((rows, features), jnp.bfloat16),
        in_specs=[hbm] * 3 + [vmem] * 5 + [hbm] * 2,
        out_specs=vmem,
        scratch_shapes=[
            pltpu.SMEM(mask.shape, jnp.int32),
            pltpu.SMEM(cols.shape, jnp.int32),
            pltpu.SMEM(count.shape, jnp.int32),
            pltpu.VMEM(dense.shape, jnp.bfloat16),
            pltpu.VMEM(sparse.shape, jnp.bfloat16),
            pltpu.VMEM((depth, features), jnp.bfloat16),
            pltpu.SemaphoreType.DMA((3,)),
            pltpu.SemaphoreType.DMA((steps,)),
            pltpu.SemaphoreType.DMA((steps,)),
        ],
        compiler_params=pltpu.CompilerParams(vmem_limit_bytes=52 * 2**20),
        cost_estimate=pl.CostEstimate(
            flops=2 * rows * depth * features, bytes_accessed=2 * rows * depth, transcendentals=0
        ),
    )(mask, cols, count, *neighbours, panel, dense, sparse)


def layer_kernel(parts_ref, weight_ref, bias_ref, cotangent_ref, out_ref, grad_ref):
    aggregated = total_of(parts_ref).astype(jnp.bfloat16)
    pre_act = jnp.dot(aggregated, weight_ref[...], preferred_element_type=jnp.float32) + bias_ref[...]
    sigmoid_part = jax.nn.sigmoid(pre_act)
    out_ref[...] = (pre_act * sigmoid_part).astype(jnp.bfloat16)
    slope = sigmoid_part * (1.0 + pre_act * (1.0 - sigmoid_part))
    grad_pre = (cotangent_ref[...].astype(jnp.float32) * slope).astype(jnp.bfloat16)
    weight_grad = lax.dot_general(
        aggregated, grad_pre, (((0,), (0,)), ((), ())), preferred_element_type=jnp.float32
    )
    bias_grad = jnp.sum(grad_pre.astype(jnp.float32), axis=0, keepdims=True)
    halves = bias_grad.shape[1] // BLK
    blocks = grad_ref.shape[0] // halves
    extra = jnp.concatenate([bias_grad[:, h * BLK : (h + 1) * BLK] for h in range(halves)], axis=0)
    extra = jnp.broadcast_to(extra[None], (blocks,) + extra.shape).astype(grad_ref.dtype)
    for half in range(halves):
        tile = weight_grad[:, half * BLK : (half + 1) * BLK].reshape(blocks, 8, BLK)
        at = slice(half * blocks, (half + 1) * blocks)
        for pair in range(4):
            lanes = slice(pair * BLK, (pair + 1) * BLK)
            grad_ref[at, :, lanes] = tile[:, 2 * pair : 2 * pair + 2, :].astype(grad_ref.dtype)
        grad_ref[at, :, 4 * BLK :] = extra


def layer(parts, weight, bias, cotangent):
    rows, features = cotangent.shape
    return pl.pallas_call(
        layer_kernel,
        out_shape=(
            jax.ShapeDtypeStruct((rows, features), jnp.bfloat16),
            jax.ShapeDtypeStruct((features // BLK * features // 8, 2, 5 * BLK), jnp.bfloat16),
        ),
        compiler_params=pltpu.CompilerParams(vmem_limit_bytes=16 * 2**20),
    )(parts, weight, bias.reshape(1, features), cotangent)


def total_of(parts_ref):
    total = parts_ref[0].astype(jnp.float32)
    for part in range(1, parts_ref.shape[0]):
        total = total + parts_ref[part].astype(jnp.float32)
    return total


def plane_kernel(parts_ref, out_ref):
    total = total_of(parts_ref).astype(out_ref.dtype)
    out_ref[...] = jnp.broadcast_to(total[None], out_ref.shape)


def depth_kernel(parts_ref, out_ref, bias_ref):
    total = total_of(parts_ref)
    pairs = out_ref.shape[1] // 2
    bias = total[:, pairs * BLK :]
    bias_ref[...] = jnp.concatenate([bias[half : half + 1] for half in range(bias.shape[0])], axis=1)
    tile = jnp.concatenate([total[:, pair * BLK : (pair + 1) * BLK] for pair in range(pairs)], axis=0)
    out_ref[...] = jnp.broadcast_to(tile.astype(out_ref.dtype)[None], out_ref.shape)


def unpack_kernel(pieces_ref, out_ref):
    for half in range(pieces_ref.shape[0]):
        tile = pieces_ref[half].astype(jnp.float32)
        out_ref[:, half * BLK : (half + 1) * BLK] = tile.reshape(out_ref.shape[0], BLK)


def exchanged(pieces, axes):
    return lax.all_to_all(pieces, axes, 0, 0, tiled=False)


def summed_over_devices(grads):
    plane, depth = lax.axis_size(PLANE), lax.axis_size(DEPTH)
    halves = 2
    blocks, features = grads.shape[0] // halves, halves * BLK
    mine = pl.pallas_call(
        plane_kernel, out_shape=jax.ShapeDtypeStruct((depth,) + grads.shape[1:], jnp.bfloat16), compiler_params=SMALL
    )(exchanged(grads, PLANE))
    mine, bias_grad = pl.pallas_call(
        depth_kernel,
        out_shape=(
            jax.ShapeDtypeStruct((plane, 8, BLK), jnp.bfloat16),
            jax.ShapeDtypeStruct((1, features), jnp.float32),
        ),
        compiler_params=SMALL,
    )(exchanged(mine, DEPTH))
    weight_grad = pl.pallas_call(
        unpack_kernel,
        out_shape=jax.ShapeDtypeStruct((blocks * 8, features), jnp.float32),
        compiler_params=SMALL,
    )(exchanged(mine, PLANE).reshape(halves, blocks, 8, BLK))
    return weight_grad, bias_grad.reshape(features)


def on_device(
    features, weight, bias, dense_adj, dense_mask, sparse_adj, sparse_cols, sparse_count, cotangent
):
    band, rows = dense_adj.shape[2], dense_adj.shape[3]
    reach = (band - 1) // 2
    width = features.shape[1]
    neighbours = [fetched_from(features, k) for k in (1, -1, -2, 2)]
    panel = lax.all_gather(features, REP, axis=0, tiled=False)
    partial = partial_sums(
        dense_mask.reshape(band, 1, rows // BLK),
        sparse_cols,
        sparse_count,
        neighbours,
        panel,
        dense_adj[0, 0],
        sparse_adj[0, 0],
    )
    shares = lax.axis_size(REP)
    parts = exchanged(partial.reshape(shares, rows // shares, width), REP)
    activated, grads = layer(parts, weight, bias, cotangent)
    weight_grad, bias_grad = summed_over_devices(grads)
    return activated, weight_grad, bias_grad


def solution(mesh):
    fine = Mesh(mesh.devices.reshape(SIZES), AXES)
    nodes = P(AXES, None)
    in_specs = (
        nodes,
        P(),
        P(),
        P(ROW, REP, None, None, None),
        P(ROW, REP, None, None, None),
        P(ROW, REP, None, None),
        P(ROW, REP, None),
        P(ROW, REP),
        nodes,
    )
    return jax.shard_map(
        on_device, mesh=fine, in_specs=in_specs, out_specs=(nodes, P(), P()), check_vma=False
    )
```
